512 devices in a mesh: section: 64 (over y, z_lo, x), tp: 8 (over z_hi, core).
Axes of the slice: x: 4, y: 4, z: 16 (z_hi: 4, z_lo: 4; z = z_hi * 4 + z_lo), core: 2. Of those that a mesh axis runs over, the one named last changes fastest.
Arguments:
- fwd_q: bfloat16 [64, 128, 8192], P('section', None, 'tp'), may hold values from -4.5 to 4.5
- fwd_k: bfloat16 [64, 128, 1024], P('section', None, 'tp'), may hold values from -4.5 to 4.5
- fwd_v: bfloat16 [64, 128, 1024], P('section', None, 'tp'), may hold values from -6 to 6
- fwd_segments: int32 [64, 128], P('section'), may hold values from 0 to 3, never falling along the last dimension, each value on 1 to 64 neighbouring positions
- held_q: bfloat16 [64, 128, 8192], P('section', None, 'tp'), may hold values from -4.5 to 4.5
- held_k: bfloat16 [64, 128, 1024], P('section', None, 'tp'), may hold values from -4.5 to 4.5
- held_v: bfloat16 [64, 128, 1024], P('section', None, 'tp'), may hold values from -6 to 6
- back_segments: int32 [64, 128], P('section'), may hold values from 0 to 3, never falling along the last dimension, each value on 1 to 64 neighbouring positions
- up_grad: bfloat16 [64, 128, 8192], P('section', None, 'tp'), may hold values from -6 to 6
Outputs:
- passed_output: bfloat16 [64, 128, 8192], P('section', 'tp')
- evicted_q: bfloat16 [64, 128, 8192], P('section', None, 'tp')
- evicted_k: bfloat16 [64, 128, 1024], P('section', None, 'tp')
- evicted_v: bfloat16 [64, 128, 1024], P('section', None, 'tp')
- grad_q: bfloat16 [64, 128, 8192], P('section', None, 'tp')
- grad_k: bfloat16 [64, 128, 1024], P('section', None, 'tp')
- grad_v: bfloat16 [64, 128, 1024], P('section', None, 'tp')
The draws below stay inside these ranges and needn't reach their ends.
Inputs may be any that keep to these rules, and one draw needn't show every extreme that they name: `fwd_segments`: document numbers never fall along a micro-batch; each document has 1 to 64 tokens. `back_segments`: document numbers never fall along a micro-batch; each document has 1 to 64 tokens.
All inputs are finite; a program needn't handle non-finite values.
Results may differ from the reference program's by a relative error of at most 0.0058.
Values may be sent and summed in bfloat16 or wider, within the bound.
No kernel may reach another device: no remote copies, remote signals or barrier semaphores. Data moves between devices by JAX's collectives and lax.ppermute only.
A program may use at most 64 MiB of HBM per device.

```python
import math
import jax
import jax.numpy as jnp
import numpy as np
from jax import lax

HQ = 64
KV = 8
HD = 128
TOKENS = 128
SECTIONS = 64


def query_values(key, fold):
    key = jax.random.fold_in(key, fold)
    values_drawn = jnp.clip(jax.random.normal(key, (SECTIONS, TOKENS, HQ * HD)), -4.5, 4.5)
    return values_drawn.astype(jnp.float32)


def key_values(key, fold):
    key = jax.random.fold_in(key, fold)
    values_drawn = jnp.clip(jax.random.normal(key, (SECTIONS, TOKENS, KV * HD)), -4.5, 4.5)
    return values_drawn.astype(jnp.float32)


def draw_fwd_q(key, part):
    return query_values(key, 1).astype(jnp.bfloat16)


def draw_fwd_k(key, part):
    return key_values(key, 2).astype(jnp.bfloat16)


def draw_held_q(key, part):
    return query_values(key, 3).astype(jnp.bfloat16)


def draw_held_k(key, part):
    return key_values(key, 4).astype(jnp.bfloat16)


def block_scale(key, extent, cuts, low, top_value):
    def one(axis_at, parts):
        steps = jax.random.uniform(jax.random.fold_in(jax.random.fold_in(key, 6), axis_at), (parts,), jnp.float32, low / len(cuts), top_value / len(cuts))
        return jnp.repeat(jnp.exp(steps), extent[axis_at] // parts).reshape((-1,) + (1,) * (len(extent) - axis_at - 1))

    gain = one(*cuts[0])
    for cut in cuts[1:]:
        gain = gain * one(*cut)
    return gain


def split_up(number_of, total, reach, lean):
    loads = [(1 << 20) // math.isqrt(grade ** lean) + 1 for grade in range(2, number_of + 1)]
    rest, counts = total - reach - (number_of - 1), [1] * (number_of - 1)
    while rest > 0:
        candidates = [i for i in range(number_of - 1) if counts[i] < reach]
        whole, budget = sum([loads[i] for i in candidates]), rest
        for i in candidates:
            addition = min(reach - counts[i], max(1, budget * loads[i] // whole), rest)
            counts[i] = counts[i] + addition
            rest = rest - addition
    return np.array([reach] + counts)


def ragged(key, count, total, reach, skew):
    if count == 2:
        one = jax.random.randint(key, (), max(1, total - reach), min(reach, total - 1) + 1)
        return jnp.stack([one, total - one])
    tallies = jnp.asarray(split_up(count, total, reach, skew), jnp.int32)
    pairs = (count - 1) // 2
    donor, taker = tallies[1:1 + 2 * pairs:2], tallies[2:2 + 2 * pairs:2]
    slack = jnp.minimum(donor - 1, reach - taker)
    moved = jax.random.randint(jax.random.fold_in(key, 1), (pairs,), 0, 1 << 20) % (slack + 1)
    tallies = tallies.at[1:1 + 2 * pairs:2].set(donor - moved).at[2:2 + 2 * pairs:2].set(taker + moved)
    return tallies[jax.random.permutation(jax.random.fold_in(key, 2), count)]


def gaussian(key, shape, width, most, pieces=(), kind=jnp.bfloat16):
    array = jax.random.normal(key, shape, jnp.float32) * width
    if len(pieces) > 0:
        array = block_scale(key, shape, pieces, -0.22, 0.18) * array
    return jnp.clip(array, min=-most, max=most).astype(kind)


def setup_inputs(seed: int = 0) -> dict:
    seeds = jax.random.split(jax.random.key(seed), 10)
    fwd_q = draw_fwd_q(jax.random.fold_in(seeds[9], 71), 0)
    fwd_k = draw_fwd_k(jax.random.fold_in(seeds[9], 71), 0)
    fwd_v = gaussian(seeds[2], (SECTIONS, TOKENS, KV * HD), 1.0, 6.0, ((0, 64), (2, 8)))
    fwd_segments = jax.vmap(lambda own: jnp.searchsorted(jnp.cumsum(ragged(own, 4, TOKENS, TOKENS // 2, 2)), jnp.arange(TOKENS), side="right"))(jax.random.split(seeds[3], SECTIONS)).reshape((SECTIONS, TOKENS)).astype(jnp.int32)
    held_q = draw_held_q(jax.random.fold_in(seeds[9], 71), 0)
    held_k = draw_held_k(jax.random.fold_in(seeds[9], 71), 0)
    held_v = gaussian(seeds[6], (SECTIONS, TOKENS, KV * HD), 1.0, 6.0, ((0, 64), (2, 8)))
    back_segments = jax.vmap(lambda own: jnp.searchsorted(jnp.cumsum(ragged(own, 4, TOKENS, TOKENS // 2, 2)), jnp.arange(TOKENS), side="right"))(jax.random.split(seeds[7], SECTIONS)).reshape((SECTIONS, TOKENS)).astype(jnp.int32)
    up_grad = gaussian(seeds[8], (SECTIONS, TOKENS, HQ * HD), 1.0, 6.0, ((0, 64), (2, 8)))
    return {"fwd_q": fwd_q, "fwd_k": fwd_k, "fwd_v": fwd_v, "fwd_segments": fwd_segments, "held_q": held_q, "held_k": held_k, "held_v": held_v, "back_segments": back_segments, "up_grad": up_grad}


def probability(query_heads, key_heads, segment_ids):
    row_count = query_heads.shape[0]
    scores = jnp.einsum("qkgd,skd->kgqs", query_heads, key_heads) * (HD ** -0.5)
    positions = jnp.arange(row_count)
    allowed = (segment_ids[:, None] == segment_ids[None, :]) & (positions[:, None] >= positions[None, :])
    scores = jnp.where(allowed, scores, -jnp.inf)
    row_max = jnp.max(scores, axis=-1, keepdims=True)
    weights = jnp.exp(scores - row_max)
    return weights / jnp.sum(weights, axis=-1, keepdims=True)


def split_heads(queries, key_rows, value_rows):
    row_count = queries.shape[0]
    group_size = HQ // KV
    query_heads = queries.astype(jnp.float32).reshape(row_count, KV, group_size, HD)
    key_heads = key_rows.astype(jnp.float32).reshape(row_count, KV, HD)
    value_heads = value_rows.astype(jnp.float32).reshape(row_count, KV, HD)
    return query_heads, key_heads, value_heads


def forward(queries, key_rows, value_rows, segment_ids):
    query_heads, key_heads, value_heads = split_heads(queries, key_rows, value_rows)
    prob = probability(query_heads, key_heads, segment_ids)
    prob_low = lax.optimization_barrier(prob.astype(jnp.bfloat16)).astype(jnp.float32)
    result = jnp.einsum("kgqs,skd->qkgd", prob_low, value_heads)
    return result.reshape(queries.shape[0], HQ * HD).astype(jnp.bfloat16)


def backward(queries, key_rows, value_rows, segment_ids, out_grad):
    row_count = queries.shape[0]
    query_heads, key_heads, value_heads = split_heads(queries, key_rows, value_rows)
    prob = probability(query_heads, key_heads, segment_ids)
    prob_low = lax.optimization_barrier(prob.astype(jnp.bfloat16)).astype(jnp.float32)
    grad_heads = out_grad.astype(jnp.float32).reshape(row_count, KV, HQ // KV, HD)
    value_grad = jnp.einsum("kgqs,qkgd->skd", prob_low, grad_heads)
    dprob = jnp.einsum("qkgd,skd->kgqs", grad_heads, value_heads)
    delta = jnp.sum(prob * dprob, axis=-1, keepdims=True)
    dscore = prob * (dprob - delta) * (HD ** -0.5)
    dscore = lax.optimization_barrier(dscore.astype(jnp.bfloat16)).astype(jnp.float32)
    query_grad = jnp.einsum("kgqs,skd->qkgd", dscore, key_heads)
    key_grad = jnp.einsum("kgqs,qkgd->skd", dscore, query_heads)
    return (query_grad.reshape(row_count, HQ * HD).astype(jnp.bfloat16),
            key_grad.reshape(row_count, KV * HD).astype(jnp.bfloat16),
            value_grad.reshape(row_count, KV * HD).astype(jnp.bfloat16))


def reference(fwd_q, fwd_k, fwd_v, fwd_segments, held_q, held_k, held_v, back_segments, up_grad):
    outputs = lax.map(lambda items: forward(*items), (fwd_q, fwd_k, fwd_v, fwd_segments))
    passed_output = jnp.roll(outputs, 1, axis=0)
    evicted_q = jnp.flip(fwd_q, axis=0)
    evicted_k = jnp.flip(fwd_k, axis=0)
    evicted_v = jnp.flip(fwd_v, axis=0)
    own_q = jnp.flip(held_q, axis=0)
    own_k = jnp.flip(held_k, axis=0)
    own_v = jnp.flip(held_v, axis=0)
    arriving = jnp.roll(up_grad, -1, axis=0)
    grad_q, grad_k, grad_v = lax.map(lambda items: backward(*items), (own_q, own_k, own_v, back_segments, arriving))
    return passed_output, evicted_q, evicted_k, evicted_v, grad_q, grad_k, grad_v
```

```python
import jax
import jax.numpy as jnp
from jax import lax
from jax.sharding import PartitionSpec as P

HQ = 64
KV = 8
HD = 128


def shifted_2(value, axis, steps):
    count = lax.axis_size(axis)
    pairs = [(source, (source + steps) % count) for source in range(count)]
    return lax.ppermute(value, axis, pairs)


def split_heads(queries, key_rows, value_rows):
    row_count = queries.shape[0]
    kv_local = key_rows.shape[1] // HD
    group_size = HQ // KV
    query_heads = queries.reshape(row_count, kv_local, group_size, HD)
    key_heads = key_rows.reshape(row_count, kv_local, HD)
    value_heads = value_rows.reshape(row_count, kv_local, HD)
    return (query_heads, key_heads, value_heads)


def probability(query_heads, key_heads, segment_ids):
    row_count = query_heads.shape[0]
    scores = jnp.einsum(
        "qkgd,skd->kgqs", query_heads, key_heads, preferred_element_type=jnp.float32
    ) * HD ** (-0.5)
    positions = jnp.arange(row_count)
    allowed = (segment_ids[:, None] == segment_ids[None, :]) & (
        positions[:, None] >= positions[None, :]
    )
    scores = jnp.where(allowed, scores, -jnp.inf)
    row_max = jnp.max(scores, axis=-1, keepdims=True)
    weights = jnp.exp(scores - row_max)
    return weights / jnp.sum(weights, axis=-1, keepdims=True)


def forward(queries, key_rows, value_rows, segment_ids):
    query_heads, key_heads, value_heads = split_heads(queries, key_rows, value_rows)
    prob = probability(query_heads, key_heads, segment_ids)
    prob_low = prob.astype(jnp.bfloat16)
    result = jnp.einsum("kgqs,skd->qkgd", prob_low, value_heads, preferred_element_type=jnp.float32)
    return result.reshape(queries.shape[0], queries.shape[1]).astype(jnp.bfloat16)


def backward(queries, key_rows, value_rows, segment_ids, out_grad):
    row_count = queries.shape[0]
    query_heads, key_heads, value_heads = split_heads(queries, key_rows, value_rows)
    prob = probability(query_heads, key_heads, segment_ids)
    prob_low = prob.astype(jnp.bfloat16)
    grad_heads = out_grad.reshape(query_heads.shape)
    value_grad = jnp.einsum(
        "kgqs,qkgd->skd", prob_low, grad_heads, preferred_element_type=jnp.float32
    )
    dprob = jnp.einsum(
        "qkgd,skd->kgqs", grad_heads, value_heads, preferred_element_type=jnp.float32
    )
    delta = jnp.sum(prob * dprob, axis=-1, keepdims=True)
    dscore = (prob * (dprob - delta) * HD ** (-0.5)).astype(jnp.bfloat16)
    query_grad = jnp.einsum("kgqs,skd->qkgd", dscore, key_heads, preferred_element_type=jnp.float32)
    key_grad = jnp.einsum("kgqs,qkgd->skd", dscore, query_heads, preferred_element_type=jnp.float32)
    return (
        query_grad.reshape(row_count, queries.shape[1]).astype(jnp.bfloat16),
        key_grad.reshape(row_count, key_rows.shape[1]).astype(jnp.bfloat16),
        value_grad.reshape(row_count, key_rows.shape[1]).astype(jnp.bfloat16),
    )


def mirror_move(stash):
    count = lax.axis_size("section")
    return lax.ppermute(stash, "section", [(i, count - 1 - i) for i in range(count)])


def shards(fwd_q, fwd_k, fwd_v, fwd_segments, held_q, held_k, held_v, back_segments, up_grad):
    query_width = fwd_q.shape[2]
    key_width = fwd_k.shape[2]
    held_stash = jnp.concatenate([held_q[0], held_k[0], held_v[0]], axis=1)
    held_stash = mirror_move(held_stash)
    out_local = forward(fwd_q[0], fwd_k[0], fwd_v[0], fwd_segments[0])
    fresh_stash = jnp.concatenate([fwd_q[0], fwd_k[0], fwd_v[0]], axis=1)
    fresh_stash = mirror_move(fresh_stash)
    arriving = shifted_2(up_grad[0], "section", -1)
    own_q = held_stash[:, :query_width]
    own_k = held_stash[:, query_width : query_width + key_width]
    own_v = held_stash[:, query_width + key_width :]
    grad_q, grad_k, grad_v = backward(own_q, own_k, own_v, back_segments[0], arriving)
    shifted = shifted_2(out_local, "section", 1)
    passed_output = lax.all_to_all(shifted, "tp", split_axis=0, concat_axis=1, tiled=True)
    evicted_q = fresh_stash[:, :query_width]
    evicted_k = fresh_stash[:, query_width : query_width + key_width]
    evicted_v = fresh_stash[:, query_width + key_width :]
    return (
        passed_output[None],
        evicted_q[None],
        evicted_k[None],
        evicted_v[None],
        grad_q[None],
        grad_k[None],
        grad_v[None],
    )


def solution(mesh):
    in_specs = (
        P("section", None, "tp"),
        P("section", None, "tp"),
        P("section", None, "tp"),
        P("section", None),
        P("section", None, "tp"),
        P("section", None, "tp"),
        P("section", None, "tp"),
        P("section", None),
        P("section", None, "tp"),
    )
    out_specs = (
        P("section", "tp", None),
        P("section", None, "tp"),
        P("section", None, "tp"),
        P("section", None, "tp"),
        P("section", None, "tp"),
        P("section", None, "tp"),
        P("section", None, "tp"),
    )
    return jax.shard_map(shards, mesh=mesh, in_specs=in_specs, out_specs=out_specs, check_vma=False)
```

```python
import jax
import jax.numpy as jnp
from jax import lax
from jax.experimental import pallas as pl
from jax.experimental.pallas import tpu as pltpu
from jax.sharding import PartitionSpec as P

HD = 128
SCALE = HD ** -0.5
VMEM = pl.BlockSpec(memory_space=pltpu.VMEM)
FORWARD_FLOPS = 4
BACKWARD_FLOPS = 100


def contract(left, right, left_dim, right_dim):
    return lax.dot_general(left, right, (((left_dim,), (right_dim,)), ((), ())), preferred_element_type=jnp.float32)


def stacked(ref, width):
    return jnp.concatenate([ref[:, start : start + HD] for start in range(0, width, HD)], axis=0)


def unstack(ref, heads):
    rows, width = ref.shape
    for head in range(width // HD):
        ref[:, head * HD : (head + 1) * HD] = heads[head * rows : (head + 1) * rows]


def probability(queries, keys, segments):
    count = segments.shape[1]
    across = jnp.broadcast_to(segments, (count, count))
    key_at = lax.broadcasted_iota(jnp.int32, (count, count), 0)
    query_at = lax.broadcasted_iota(jnp.int32, (count, count), 1)
    allowed = (across == across.T) & (key_at <= query_at)
    allowed = jnp.concatenate([allowed] * (queries.shape[0] // count), axis=1)
    scores = jnp.where(allowed, contract(keys, queries, 1, 1) * SCALE, -jnp.inf)
    weights = jnp.exp(scores - jnp.max(scores, axis=0, keepdims=True))
    return weights * (1.0 / jnp.sum(weights, axis=0, keepdims=True))


def forward_kernel(q_ref, k_ref, v_ref, segments_ref, out_ref):
    prob = probability(stacked(q_ref, q_ref.shape[1]), k_ref[...], segments_ref[...])
    unstack(out_ref, contract(prob.astype(jnp.bfloat16), v_ref[...], 0, 0).astype(jnp.bfloat16))


def backward_kernel(stash_ref, grad_ref, segments_ref, grad_q_ref, grad_k_ref, grad_v_ref):
    width = grad_ref.shape[1]
    queries, grads = stacked(stash_ref, width), stacked(grad_ref, width)
    keys, values = stash_ref[:, width : width + HD], stash_ref[:, width + HD :]
    prob = probability(queries, keys, segments_ref[...])
    dprob = contract(values, grads, 1, 1)
    delta = jnp.sum(prob * dprob, axis=0, keepdims=True)
    dscore = (prob * (dprob - delta) * SCALE).astype(jnp.bfloat16)
    grad_v_ref[...] = contract(prob.astype(jnp.bfloat16), grads, 1, 0).astype(jnp.bfloat16)
    grad_k_ref[...] = contract(dscore, queries, 1, 0).astype(jnp.bfloat16)
    unstack(grad_q_ref, contract(dscore, keys, 0, 0).astype(jnp.bfloat16))


def like(rows, columns):
    return jax.ShapeDtypeStruct((rows, columns), jnp.bfloat16)


def forward(q, k, v, segments):
    rows, width = q.shape
    return pl.pallas_call(
        forward_kernel,
        out_shape=like(rows, width),
        in_specs=[VMEM] * 4,
        out_specs=VMEM,
        cost_estimate=pl.CostEstimate(flops=FORWARD_FLOPS * rows * rows * width, bytes_accessed=8 * rows * width, transcendentals=rows * width),
        name="forward",
    )(q, k, v, segments)


def backward(stash, grad, segments):
    rows, width = grad.shape
    return pl.pallas_call(
        backward_kernel,
        out_shape=(like(rows, width), like(rows, HD), like(rows, HD)),
        in_specs=[VMEM] * 3,
        out_specs=(VMEM, VMEM, VMEM),
        cost_estimate=pl.CostEstimate(flops=BACKWARD_FLOPS * rows * rows * width, bytes_accessed=8 * rows * width, transcendentals=rows * width),
        name="backward",
    )(stash, grad, segments)


def shifted(value, steps):
    count = lax.axis_size("section")
    return lax.ppermute(value, "section", [(i, (i + steps) % count) for i in range(count)])


def mirrored(value):
    count = lax.axis_size("section")
    return lax.ppermute(value, "section", [(i, count - 1 - i) for i in range(count)])


def shards(fwd_q, fwd_k, fwd_v, fwd_segments, held_q, held_k, held_v, back_segments, up_grad):
    width = fwd_q.shape[2]
    held = mirrored(jnp.concatenate([held_q[0], held_k[0], held_v[0]], axis=1))
    out = forward(fwd_q[0], fwd_k[0], fwd_v[0], fwd_segments)
    fresh = mirrored(jnp.concatenate([fwd_q[0], fwd_k[0], fwd_v[0]], axis=1))
    out = shifted(out, 1)
    arriving = shifted(up_grad[0], -1)
    passed = lax.all_to_all(out, "tp", split_axis=0, concat_axis=1, tiled=True)
    grad_q, grad_k, grad_v = backward(held, arriving, back_segments)
    evicted = fresh[:, :width], fresh[:, width : width + HD], fresh[:, width + HD :]
    return tuple(x[None] for x in (passed, *evicted, grad_q, grad_k, grad_v))


def solution(mesh):
    heads, tokens = P("section", None, "tp"), P("section", "tp", None)
    segments = P("section", None)
    in_specs = (heads, heads, heads, segments, heads, heads, heads, segments, heads)
    out_specs = (tokens, heads, heads, heads, heads, heads, heads)
    return jax.shard_map(shards, mesh=mesh, in_specs=in_specs, out_specs=out_specs, check_vma=False)
```

```python
import jax
import jax.numpy as jnp
from jax import lax
from jax.experimental import pallas as pl
from jax.experimental.pallas import tpu as pltpu
from jax.sharding import PartitionSpec as P

HD = 128
SCALE = HD ** -0.5
VMEM = pl.BlockSpec(memory_space=pltpu.VMEM)
FORWARD_FLOPS = 4
BACKWARD_FLOPS = 300


def contract(left, right, left_dim, right_dim):
    return lax.dot_general(left, right, (((left_dim,), (right_dim,)), ((), ())), preferred_element_type=jnp.float32)


def stacked(ref, width):
    return jnp.concatenate([ref[:, start : start + HD] for start in range(0, width, HD)], axis=0)


def unstack(ref, heads):
    rows, width = ref.shape
    for head in range(width // HD):
        ref[:, head * HD : (head + 1) * HD] = heads[head * rows : (head + 1) * rows]


def probability(queries, keys, segments):
    count = segments.shape[1]
    across = jnp.broadcast_to(segments, (count, count))
    key_at = lax.broadcasted_iota(jnp.int32, (count, count), 0)
    query_at = lax.broadcasted_iota(jnp.int32, (count, count), 1)
    allowed = (across == across.T) & (key_at <= query_at)
    allowed = jnp.concatenate([allowed] * (queries.shape[0] // count), axis=1)
    scores = jnp.where(allowed, contract(keys, queries, 1, 1) * SCALE, -jnp.inf)
    weights = jnp.exp(scores - jnp.max(scores, axis=0, keepdims=True))
    return weights * (1.0 / jnp.sum(weights, axis=0, keepdims=True))


def forward_kernel(q_ref, k_ref, v_ref, segments_ref, held_q_ref, held_k_ref, held_v_ref, out_ref, stash_ref):
    rows, width = q_ref.shape
    prob = probability(stacked(q_ref, width), k_ref[...], segments_ref[...])
    stash_ref[:, :width] = held_q_ref[...]
    stash_ref[:, width : width + HD] = held_k_ref[...]
    stash_ref[:, width + HD : width + 2 * HD] = held_v_ref[...]
    whole = width + 2 * HD
    stash_ref[:, whole : whole + HD] = k_ref[...]
    stash_ref[:, whole + HD :] = v_ref[...]
    unstack(out_ref, contract(prob.astype(jnp.bfloat16), v_ref[...], 0, 0).astype(jnp.bfloat16))


def backward_kernel(stash_ref, grad_ref, segments_ref, grad_q_ref, grad_k_ref, grad_v_ref, fresh_k_ref, fresh_v_ref):
    width = grad_ref.shape[1]
    fresh_k_ref[...] = stash_ref[:, width + 2 * HD : width + 3 * HD]
    fresh_v_ref[...] = stash_ref[:, width + 3 * HD :]
    queries, grads = stacked(stash_ref, width), stacked(grad_ref, width)
    keys, values = stash_ref[:, width : width + HD], stash_ref[:, width + HD : width + 2 * HD]
    prob = probability(queries, keys, segments_ref[...])
    dprob = contract(values, grads, 1, 1)
    delta = jnp.sum(prob * dprob, axis=0, keepdims=True)
    dscore = (prob * (dprob - delta) * SCALE).astype(jnp.bfloat16)
    grad_v_ref[...] = contract(prob.astype(jnp.bfloat16), grads, 1, 0).astype(jnp.bfloat16)
    grad_k_ref[...] = contract(dscore, queries, 1, 0).astype(jnp.bfloat16)
    unstack(grad_q_ref, contract(dscore, keys, 0, 0).astype(jnp.bfloat16))


def like(rows, columns):
    return jax.ShapeDtypeStruct((rows, columns), jnp.bfloat16)


def forward(q, k, v, segments, held_q, held_k, held_v):
    rows, width = q.shape
    whole = width + 2 * HD
    return pl.pallas_call(
        forward_kernel,
        out_shape=(like(rows, width), like(rows, whole + 2 * HD)),
        in_specs=[VMEM] * 7,
        out_specs=(VMEM,) * 2,
        cost_estimate=pl.CostEstimate(flops=FORWARD_FLOPS * rows * rows * width, bytes_accessed=20 * rows * width, transcendentals=rows * width),
        name="forward",
    )(q, k, v, segments, held_q, held_k, held_v)


def backward(stash, grad, segments):
    rows, width = grad.shape
    return pl.pallas_call(
        backward_kernel,
        out_shape=(like(rows, width),) + (like(rows, HD),) * 4,
        in_specs=[VMEM] * 3,
        out_specs=(VMEM,) * 5,
        cost_estimate=pl.CostEstimate(flops=BACKWARD_FLOPS * rows * rows * width, bytes_accessed=8 * rows * width, transcendentals=rows * width),
        name="backward",
    )(stash, grad, segments)


def shifted(value, steps):
    count = lax.axis_size("section")
    return lax.ppermute(value, "section", [(i, (i + steps) % count) for i in range(count)])


def mirrored(value, lines=None):
    count, parts = lax.axis_size("section"), lax.axis_size("tp")
    if lines is None:
        return lax.ppermute(value, "section", [(i, count - 1 - i) for i in range(count)])
    pairs = [(i * parts + t, (count - 1 - i) * parts + t) for i in range(count) for t in range(parts) if t // 2 in lines]
    return lax.ppermute(value, ("section", "tp"), pairs)


def shards(fwd_q, fwd_k, fwd_v, fwd_segments, held_q, held_k, held_v, back_segments, up_grad):
    arriving = shifted(up_grad[0], -1)
    out, stash = forward(fwd_q[0], fwd_k[0], fwd_v[0], fwd_segments, held_q[0], held_k[0], held_v[0])
    out = shifted(out, 1)
    stash = mirrored(stash)
    lines = range(lax.axis_size("tp") // 2)
    early_q = mirrored(fwd_q[0], lines[:1])
    passed = lax.all_to_all(out, "tp", split_axis=0, concat_axis=1, tiled=True)
    late_q = mirrored(fwd_q[0], lines[1:])
    stash, early_q = lax.optimization_barrier((stash, early_q))
    grad_q, grad_k, grad_v, evicted_k, evicted_v = backward(stash, arriving, back_segments)
    late_q, grad_k = lax.optimization_barrier((late_q, grad_k))
    evicted_q = jnp.where(lax.axis_index("tp") < 2, early_q, late_q)
    return tuple(x[None] for x in (passed, evicted_q, evicted_k, evicted_v, grad_q, grad_k, grad_v))


def solution(mesh):
    heads, tokens = P("section", None, "tp"), P("section", "tp", None)
    segments = P("section", None)
    in_specs = (heads, heads, heads, segments, heads, heads, heads, segments, heads)
    out_specs = (tokens, heads, heads, heads, heads, heads, heads)
    return jax.shard_map(shards, mesh=mesh, in_specs=in_specs, out_specs=out_specs, check_vma=False)
```

```python
import jax
import jax.numpy as jnp
from jax import lax
from jax.experimental import pallas as pl
from jax.experimental.pallas import tpu as pltpu
from jax.sharding import PartitionSpec as P

HD = 128
SCALE = HD ** -0.5
VMEM = pl.BlockSpec(memory_space=pltpu.VMEM)
FORWARD_FLOPS = 4
BACKWARD_FLOPS = 300


def contract(left, right, left_dim, right_dim):
    return lax.dot_general(left, right, (((left_dim,), (right_dim,)), ((), ())), preferred_element_type=jnp.float32)


def stacked(ref, width):
    return jnp.concatenate([ref[:, start : start + HD] for start in range(0, width, HD)], axis=0)


def unstack(ref, heads):
    rows, width = ref.shape
    for head in range(width // HD):
        ref[:, head * HD : (head + 1) * HD] = heads[head * rows : (head + 1) * rows]


def probability(queries, keys, segments):
    count = segments.shape[1]
    across = jnp.broadcast_to(segments, (count, count))
    key_at = lax.broadcasted_iota(jnp.int32, (count, count), 0)
    query_at = lax.broadcasted_iota(jnp.int32, (count, count), 1)
    allowed = (across == across.T) & (key_at <= query_at)
    allowed = jnp.concatenate([allowed] * (queries.shape[0] // count), axis=1)
    scores = jnp.where(allowed, contract(keys, queries, 1, 1) * SCALE, -jnp.inf)
    weights = jnp.exp(scores - jnp.max(scores, axis=0, keepdims=True))
    return weights * (1.0 / jnp.sum(weights, axis=0, keepdims=True))


def forward_kernel(q_ref, k_ref, v_ref, segments_ref, held_q_ref, held_k_ref, held_v_ref, out_ref, stash_ref):
    rows, width = q_ref.shape
    prob = probability(stacked(q_ref, width), k_ref[...], segments_ref[...])
    stash_ref[:, :width] = held_q_ref[...]
    stash_ref[:, width : width + HD] = held_k_ref[...]
    stash_ref[:, width + HD : width + 2 * HD] = held_v_ref[...]
    whole = width + 2 * HD
    stash_ref[:, whole : whole + HD] = k_ref[...]
    stash_ref[:, whole + HD :] = v_ref[...]
    unstack(out_ref, contract(prob.astype(jnp.bfloat16), v_ref[...], 0, 0).astype(jnp.bfloat16))


def backward_kernel(stash_ref, grad_ref, segments_ref, grad_q_ref, grad_k_ref, grad_v_ref, fresh_k_ref, fresh_v_ref):
    width = grad_ref.shape[1]
    fresh_k_ref[...] = stash_ref[:, width + 2 * HD : width + 3 * HD]
    fresh_v_ref[...] = stash_ref[:, width + 3 * HD :]
    queries, grads = stacked(stash_ref, width), stacked(grad_ref, width)
    keys, values = stash_ref[:, width : width + HD], stash_ref[:, width + HD : width + 2 * HD]
    prob = probability(queries, keys, segments_ref[...])
    dprob = contract(values, grads, 1, 1)
    delta = jnp.sum(prob * dprob, axis=0, keepdims=True)
    dscore = (prob * (dprob - delta) * SCALE).astype(jnp.bfloat16)
    grad_v_ref[...] = contract(prob.astype(jnp.bfloat16), grads, 1, 0).astype(jnp.bfloat16)
    grad_k_ref[...] = contract(dscore, queries, 1, 0).astype(jnp.bfloat16)
    unstack(grad_q_ref, contract(dscore, keys, 0, 0).astype(jnp.bfloat16))


def like(rows, columns):
    return jax.ShapeDtypeStruct((rows, columns), jnp.bfloat16)


def held_in_vmem(rows, columns):
    return pltpu.VMEM((rows, columns), jnp.bfloat16)


def forward(q, k, v, segments, held_q, held_k, held_v):
    rows, width = q.shape
    whole = width + 2 * HD
    return pl.pallas_call(
        forward_kernel,
        out_shape=(held_in_vmem(rows, width), held_in_vmem(rows, whole + 2 * HD)),
        in_specs=[VMEM] * 7,
        out_specs=(VMEM,) * 2,
        cost_estimate=pl.CostEstimate(flops=FORWARD_FLOPS * rows * rows * width, bytes_accessed=20 * rows * width, transcendentals=rows * width),
        name="forward",
    )(q, k, v, segments, held_q, held_k, held_v)


def backward(stash, grad, segments):
    rows, width = grad.shape
    return pl.pallas_call(
        backward_kernel,
        out_shape=(like(rows, width),) + (like(rows, HD),) * 4,
        in_specs=[VMEM] * 3,
        out_specs=(VMEM,) * 5,
        cost_estimate=pl.CostEstimate(flops=BACKWARD_FLOPS * rows * rows * width, bytes_accessed=8 * rows * width, transcendentals=rows * width),
        name="backward",
    )(pltpu.with_memory_space_constraint(stash, pltpu.VMEM), pltpu.with_memory_space_constraint(grad, pltpu.VMEM), segments)


def shifted(value, steps):
    count = lax.axis_size("section")
    return lax.ppermute(value, "section", [(i, (i + steps) % count) for i in range(count)])


def mirrored(value, lines=None):
    count, parts = lax.axis_size("section"), lax.axis_size("tp")
    if lines is None:
        return lax.ppermute(value, "section", [(i, count - 1 - i) for i in range(count)])
    pairs = [(i * parts + t, (count - 1 - i) * parts + t) for i in range(count) for t in range(parts) if t // 2 in lines]
    return lax.ppermute(value, ("section", "tp"), pairs)


def shards(fwd_q, fwd_k, fwd_v, fwd_segments, held_q, held_k, held_v, back_segments, up_grad):
    arriving = shifted(up_grad[0], -1)
    out, stash = forward(fwd_q[0], fwd_k[0], fwd_v[0], fwd_segments, held_q[0], held_k[0], held_v[0])
    out = shifted(out, 1)
    stash = mirrored(stash)
    lines = range(lax.axis_size("tp") // 2)
    early_q = mirrored(fwd_q[0], lines[:1])
    passed = lax.all_to_all(out, "tp", split_axis=0, concat_axis=1, tiled=True)
    late_q = mirrored(fwd_q[0], lines[1:])
    stash, early_q = lax.optimization_barrier((stash, early_q))
    grad_q, grad_k, grad_v, evicted_k, evicted_v = backward(stash, arriving, back_segments)
    late_q, grad_k = lax.optimization_barrier((late_q, grad_k))
    evicted_q = jnp.where(lax.axis_index("tp") < 2, early_q, late_q)
    return tuple(x[None] for x in (passed, evicted_q, evicted_k, evicted_v, grad_q, grad_k, grad_v))


def solution(mesh):
    heads, tokens = P("section", None, "tp"), P("section", "tp", None)
    segments = P("section", None)
    in_specs = (heads, heads, heads, segments, heads, heads, heads, segments, heads)
    out_specs = (tokens, heads, heads, heads, heads, heads, heads)
    return jax.shard_map(shards, mesh=mesh, in_specs=in_specs, out_specs=out_specs, check_vma=False)
```

```python
import jax
import jax.numpy as jnp
from jax import lax
from jax.experimental import pallas as pl
from jax.experimental.pallas import tpu as pltpu
from jax.sharding import PartitionSpec as P

HD = 128
SCALE = HD ** -0.5
VMEM = pl.BlockSpec(memory_space=pltpu.VMEM)
FORWARD_FLOPS = 4
BACKWARD_FLOPS = 450


def contract(left, right, left_dim, right_dim):
    return lax.dot_general(left, right, (((left_dim,), (right_dim,)), ((), ())), preferred_element_type=jnp.float32)


def stacked(ref, width):
    return jnp.concatenate([ref[:, start : start + HD] for start in range(0, width, HD)], axis=0)


def unstack(ref, heads):
    rows, width = ref.shape
    for head in range(width // HD):
        ref[:, head * HD : (head + 1) * HD] = heads[head * rows : (head + 1) * rows]


def probability(queries, keys, segments):
    count = segments.shape[1]
    across = jnp.broadcast_to(segments, (count, count))
    key_at = lax.broadcasted_iota(jnp.int32, (count, count), 0)
    query_at = lax.broadcasted_iota(jnp.int32, (count, count), 1)
    allowed = (across == across.T) & (key_at <= query_at)
    allowed = jnp.concatenate([allowed] * (queries.shape[0] // count), axis=1)
    scores = jnp.where(allowed, contract(keys, queries, 1, 1) * SCALE, -jnp.inf)
    weights = jnp.exp(scores - jnp.max(scores, axis=0, keepdims=True))
    return weights * (1.0 / jnp.sum(weights, axis=0, keepdims=True))


def forward_kernel(q_ref, k_ref, v_ref, segments_ref, held_q_ref, held_k_ref, held_v_ref, out_ref, stash_ref, fresh_ref):
    rows, width = q_ref.shape
    prob = probability(stacked(q_ref, width), k_ref[...], segments_ref[...])
    stash_ref[:, :width] = held_q_ref[...]
    stash_ref[:, width : width + HD] = held_k_ref[...]
    stash_ref[:, width + HD :] = held_v_ref[...]
    fresh_ref[:, :HD] = k_ref[...]
    fresh_ref[:, HD:] = v_ref[...]
    unstack(out_ref, contract(prob.astype(jnp.bfloat16), v_ref[...], 0, 0).astype(jnp.bfloat16))


def backward_kernel(stash_ref, grad_ref, segments_ref, grad_q_ref, grad_k_ref, grad_v_ref):
    width = grad_ref.shape[1]
    queries, grads = stacked(stash_ref, width), stacked(grad_ref, width)
    keys, values = stash_ref[:, width : width + HD], stash_ref[:, width + HD :]
    prob = probability(queries, keys, segments_ref[...])
    dprob = contract(values, grads, 1, 1)
    delta = jnp.sum(prob * dprob, axis=0, keepdims=True)
    dscore = (prob * (dprob - delta) * SCALE).astype(jnp.bfloat16)
    grad_v_ref[...] = contract(prob.astype(jnp.bfloat16), grads, 1, 0).astype(jnp.bfloat16)
    grad_k_ref[...] = contract(dscore, queries, 1, 0).astype(jnp.bfloat16)
    unstack(grad_q_ref, contract(dscore, keys, 0, 0).astype(jnp.bfloat16))


def like(rows, columns):
    return jax.ShapeDtypeStruct((rows, columns), jnp.bfloat16)


def finish_kernel(pieces_ref, early_ref, late_ref, fresh_ref, passed_ref, q_ref, k_ref, v_ref):
    parts, _, width = pieces_ref.shape
    late = jnp.where(lax.rem(lax.axis_index("section"), 16) == 0, parts - 2, 0)
    for part in range(parts):
        column = pl.multiple_of(lax.rem(part + late, parts) * width, width)
        passed_ref[:, pl.ds(column, width)] = pieces_ref[part]
    k_ref[...] = fresh_ref[:, :HD]
    v_ref[...] = fresh_ref[:, HD:]
    is_early = lax.axis_index("tp") < 2

    @pl.when(is_early)
    def _():
        q_ref[...] = early_ref[...]

    @pl.when(jnp.logical_not(is_early))
    def _():
        q_ref[...] = late_ref[...]


def finish(pieces, early, late, fresh):
    parts, rows, width = pieces.shape
    tokens = early.shape[0]
    arrays = (pltpu.with_memory_space_constraint(x, pltpu.VMEM) for x in (pieces, early, late, fresh))
    return pl.pallas_call(
        finish_kernel,
        out_shape=(like(rows, parts * width), like(tokens, width), like(tokens, HD), like(tokens, HD)),
        in_specs=[VMEM] * 4,
        out_specs=(VMEM,) * 4,
        cost_estimate=pl.CostEstimate(flops=0, bytes_accessed=8 * parts * rows * width, transcendentals=0),
        name="finish",
    )(*arrays)


def handed_on(value):
    count, parts = lax.axis_size("section"), lax.axis_size("tp")
    pairs = []
    for section in range(count):
        after = (section + 1) % count
        late = {0: 2}.get(after % 16, 0)
        pairs += [(section * parts + t, after * parts + (t + late) % parts) for t in range(parts)]
    return lax.ppermute(value, ("section", "tp"), pairs)


def held_in_vmem(rows, columns):
    return pltpu.VMEM((rows, columns), jnp.bfloat16)


def forward(q, k, v, segments, held_q, held_k, held_v):
    rows, width = q.shape
    whole = width + 2 * HD
    return pl.pallas_call(
        forward_kernel,
        out_shape=(held_in_vmem(rows, width), held_in_vmem(rows, whole), held_in_vmem(rows, 2 * HD)),
        in_specs=[VMEM] * 7,
        out_specs=(VMEM,) * 3,
        cost_estimate=pl.CostEstimate(flops=FORWARD_FLOPS * rows * rows * width, bytes_accessed=20 * rows * width, transcendentals=rows * width),
        name="forward",
    )(q, k, v, segments, held_q, held_k, held_v)


def backward(stash, grad, segments):
    rows, width = grad.shape
    return pl.pallas_call(
        backward_kernel,
        out_shape=(like(rows, width),) + (like(rows, HD),) * 2,
        in_specs=[VMEM] * 3,
        out_specs=(VMEM,) * 3,
        cost_estimate=pl.CostEstimate(flops=BACKWARD_FLOPS * rows * rows * width, bytes_accessed=8 * rows * width, transcendentals=rows * width),
        name="backward",
    )(pltpu.with_memory_space_constraint(stash, pltpu.VMEM), pltpu.with_memory_space_constraint(grad, pltpu.VMEM), segments)


def shifted(value, steps):
    count = lax.axis_size("section")
    return lax.ppermute(value, "section", [(i, (i + steps) % count) for i in range(count)])


def mirrored(value, lines=None):
    count, parts = lax.axis_size("section"), lax.axis_size("tp")
    if lines is None:
        return lax.ppermute(value, "section", [(i, count - 1 - i) for i in range(count)])
    pairs = [(i * parts + t, (count - 1 - i) * parts + t) for i in range(count) for t in range(parts) if t // 2 in lines]
    return lax.ppermute(value, ("section", "tp"), pairs)


def shards(fwd_q, fwd_k, fwd_v, fwd_segments, held_q, held_k, held_v, back_segments, up_grad):
    arriving = shifted(up_grad[0], -1)
    out, stash, fresh = forward(fwd_q[0], fwd_k[0], fwd_v[0], fwd_segments, held_q[0], held_k[0], held_v[0])
    parts = lax.axis_size("tp")
    out = handed_on(out).reshape(parts, out.shape[0] // parts, out.shape[1])
    stash = mirrored(stash)
    lines = range(lax.axis_size("tp") // 2)
    early_q = mirrored(fwd_q[0], lines[:1])
    pieces = lax.all_to_all(out, "tp", split_axis=0, concat_axis=0)
    late_q = mirrored(fwd_q[0], lines[1:])
    stash, early_q = lax.optimization_barrier((stash, early_q))
    grad_q, grad_k, grad_v = backward(stash, arriving, back_segments)
    late_q, fresh, grad_k = lax.optimization_barrier((late_q, mirrored(fresh), grad_k))
    passed, evicted_q, evicted_k, evicted_v = finish(pieces, early_q, late_q, fresh)
    return tuple(x[None] for x in (passed, evicted_q, evicted_k, evicted_v, grad_q, grad_k, grad_v))


def solution(mesh):
    heads, tokens = P("section", None, "tp"), P("section", "tp", None)
    segments = P("section", None)
    in_specs = (heads, heads, heads, segments, heads, heads, heads, segments, heads)
    out_specs = (tokens, heads, heads, heads, heads, heads, heads)
    return jax.shard_map(shards, mesh=mesh, in_specs=in_specs, out_specs=out_specs, check_vma=False)
```

```python
import jax
import jax.numpy as jnp
from jax import lax
from jax.experimental import pallas as pl
from jax.experimental.pallas import tpu as pltpu
from jax.sharding import PartitionSpec as P

HD = 128
SCALE = HD ** -0.5
VMEM = pl.BlockSpec(memory_space=pltpu.VMEM)
FORWARD_FLOPS = 4
BACKWARD_FLOPS = 450


def contract(left, right, left_dim, right_dim):
    return lax.dot_general(left, right, (((left_dim,), (right_dim,)), ((), ())), preferred_element_type=jnp.float32)


def stacked(ref, width):
    return jnp.concatenate([ref[:, start : start + HD] for start in range(0, width, HD)], axis=0)


def unstack(ref, heads):
    rows, width = ref.shape
    for head in range(width // HD):
        ref[:, head * HD : (head + 1) * HD] = heads[head * rows : (head + 1) * rows]


def probability(queries, keys, segments):
    count = segments.shape[1]
    across = jnp.broadcast_to(segments, (count, count))
    key_at = lax.broadcasted_iota(jnp.int32, (count, count), 0)
    query_at = lax.broadcasted_iota(jnp.int32, (count, count), 1)
    allowed = (across == across.T) & (key_at <= query_at)
    allowed = jnp.concatenate([allowed] * (queries.shape[0] // count), axis=1)
    scores = jnp.where(allowed, contract(keys, queries, 1, 1) * SCALE, -jnp.inf)
    weights = jnp.exp(scores - jnp.max(scores, axis=0, keepdims=True))
    return weights * (1.0 / jnp.sum(weights, axis=0, keepdims=True))


def forward_kernel(q_ref, k_ref, v_ref, segments_ref, held_q_ref, held_k_ref, held_v_ref, out_ref, stash_ref, fresh_ref, semaphores):
    rows, width = q_ref.shape
    copies, start = [], 0
    for index, source in enumerate((held_q_ref, held_k_ref, held_v_ref)):
        target = stash_ref.at[:, pl.ds(start, source.shape[1])]
        copies.append(pltpu.make_async_copy(source, target, semaphores.at[index]))
        copies[-1].start()
        start = start + source.shape[1]
    prob = probability(stacked(q_ref, width), k_ref[...], segments_ref[...])
    fresh_ref[:, :HD] = k_ref[...]
    fresh_ref[:, HD:] = v_ref[...]
    unstack(out_ref, contract(prob.astype(jnp.bfloat16), v_ref[...], 0, 0).astype(jnp.bfloat16))
    for copy in copies:
        copy.wait()


def backward_kernel(stash_ref, grad_ref, segments_ref, grad_q_ref, grad_k_ref, grad_v_ref):
    width = grad_ref.shape[1]
    queries, grads = stacked(stash_ref, width), stacked(grad_ref, width)
    keys, values = stash_ref[:, width : width + HD], stash_ref[:, width + HD :]
    prob = probability(queries, keys, segments_ref[...])
    dprob = contract(values, grads, 1, 1)
    delta = jnp.sum(prob * dprob, axis=0, keepdims=True)
    dscore = (prob * (dprob - delta) * SCALE).astype(jnp.bfloat16)
    grad_v_ref[...] = contract(prob.astype(jnp.bfloat16), grads, 1, 0).astype(jnp.bfloat16)
    grad_k_ref[...] = contract(dscore, queries, 1, 0).astype(jnp.bfloat16)
    unstack(grad_q_ref, contract(dscore, keys, 0, 0).astype(jnp.bfloat16))


def like(rows, columns):
    return jax.ShapeDtypeStruct((rows, columns), jnp.bfloat16)


def finish_kernel(pieces_ref, early_ref, late_ref, fresh_ref, passed_ref, q_ref, k_ref, v_ref):
    parts, _, width = pieces_ref.shape
    late = jnp.where(lax.rem(lax.axis_index("section"), 16) == 0, parts - 2, 0)
    for part in range(parts):
        column = pl.multiple_of(lax.rem(part + late, parts) * width, width)
        passed_ref[:, pl.ds(column, width)] = pieces_ref[part]
    k_ref[...] = fresh_ref[:, :HD]
    v_ref[...] = fresh_ref[:, HD:]
    is_early = lax.axis_index("tp") < 2

    @pl.when(is_early)
    def _():
        q_ref[...] = early_ref[...]

    @pl.when(jnp.logical_not(is_early))
    def _():
        q_ref[...] = late_ref[...]


def finish(pieces, early, late, fresh):
    parts, rows, width = pieces.shape
    tokens = early.shape[0]
    arrays = (pltpu.with_memory_space_constraint(x, pltpu.VMEM) for x in (pieces, early, late, fresh))
    return pl.pallas_call(
        finish_kernel,
        out_shape=(like(rows, parts * width), like(tokens, width), like(tokens, HD), like(tokens, HD)),
        in_specs=[VMEM] * 4,
        out_specs=(VMEM,) * 4,
        cost_estimate=pl.CostEstimate(flops=0, bytes_accessed=8 * parts * rows * width, transcendentals=0),
        name="finish",
    )(*arrays)


def handed_on(value):
    count, parts = lax.axis_size("section"), lax.axis_size("tp")
    pairs = []
    for section in range(count):
        after = (section + 1) % count
        late = {0: 2}.get(after % 16, 0)
        pairs += [(section * parts + t, after * parts + (t + late) % parts) for t in range(parts)]
    return lax.ppermute(value, ("section", "tp"), pairs)


def held_in_vmem(rows, columns):
    return pltpu.VMEM((rows, columns), jnp.bfloat16)


def forward(q, k, v, segments, held_q, held_k, held_v):
    rows, width = q.shape
    whole = width + 2 * HD
    return pl.pallas_call(
        forward_kernel,
        out_shape=(held_in_vmem(rows, width), held_in_vmem(rows, whole), held_in_vmem(rows, 2 * HD)),
        in_specs=[VMEM] * 4 + [pl.BlockSpec(memory_space=pl.ANY)] * 3,
        out_specs=(VMEM,) * 3,
        scratch_shapes=[pltpu.SemaphoreType.DMA((3,))],
        cost_estimate=pl.CostEstimate(flops=FORWARD_FLOPS * rows * rows * width, bytes_accessed=20 * rows * width, transcendentals=rows * width),
        name="forward",
    )(q, k, v, segments, held_q, held_k, held_v)


def backward(stash, grad, segments):
    rows, width = grad.shape
    return pl.pallas_call(
        backward_kernel,
        out_shape=(like(rows, width),) + (like(rows, HD),) * 2,
        in_specs=[VMEM] * 3,
        out_specs=(VMEM,) * 3,
        cost_estimate=pl.CostEstimate(flops=BACKWARD_FLOPS * rows * rows * width, bytes_accessed=8 * rows * width, transcendentals=rows * width),
        name="backward",
    )(pltpu.with_memory_space_constraint(stash, pltpu.VMEM), pltpu.with_memory_space_constraint(grad, pltpu.VMEM), segments)


def shifted(value, steps):
    count = lax.axis_size("section")
    return lax.ppermute(value, "section", [(i, (i + steps) % count) for i in range(count)])


def mirrored(value, lines=None):
    count, parts = lax.axis_size("section"), lax.axis_size("tp")
    if lines is None:
        return lax.ppermute(value, "section", [(i, count - 1 - i) for i in range(count)])
    pairs = [(i * parts + t, (count - 1 - i) * parts + t) for i in range(count) for t in range(parts) if t // 2 in lines]
    return lax.ppermute(value, ("section", "tp"), pairs)


def shards(fwd_q, fwd_k, fwd_v, fwd_segments, held_q, held_k, held_v, back_segments, up_grad):
    arriving = shifted(up_grad[0], -1)
    out, stash, fresh = forward(fwd_q[0], fwd_k[0], fwd_v[0], fwd_segments, held_q[0], held_k[0], held_v[0])
    parts = lax.axis_size("tp")
    out = handed_on(out).reshape(parts, out.shape[0] // parts, out.shape[1])
    stash = mirrored(stash)
    lines = range(lax.axis_size("tp") // 2)
    early_q = mirrored(fwd_q[0], lines[:1])
    pieces = lax.all_to_all(out, "tp", split_axis=0, concat_axis=0)
    late_q = mirrored(fwd_q[0], lines[1:])
    stash, early_q = lax.optimization_barrier((stash, early_q))
    grad_q, grad_k, grad_v = backward(stash, arriving, back_segments)
    late_q, fresh, grad_k = lax.optimization_barrier((late_q, mirrored(fresh), grad_k))
    passed, evicted_q, evicted_k, evicted_v = finish(pieces, early_q, late_q, fresh)
    return tuple(x[None] for x in (passed, evicted_q, evicted_k, evicted_v, grad_q, grad_k, grad_v))


def solution(mesh):
    heads, tokens = P("section", None, "tp"), P("section", "tp", None)
    segments = P("section", None)
    in_specs = (heads, heads, heads, segments, heads, heads, heads, segments, heads)
    out_specs = (tokens, heads, heads, heads, heads, heads, heads)
    return jax.shard_map(shards, mesh=mesh, in_specs=in_specs, out_specs=out_specs, check_vma=False)
```

```python
import jax
import jax.numpy as jnp
from jax import lax
from jax.experimental import pallas as pl
from jax.experimental.pallas import tpu as pltpu
from jax.sharding import PartitionSpec as P

HD = 128
SCALE = HD ** -0.5
VMEM = pl.BlockSpec(memory_space=pltpu.VMEM)
FORWARD_FLOPS = 4
BACKWARD_FLOPS = 450


def contract(left, right, left_dim, right_dim):
    return lax.dot_general(left, right, (((left_dim,), (right_dim,)), ((), ())), preferred_element_type=jnp.float32)


def stacked(ref, width):
    return jnp.concatenate([ref[:, start : start + HD] for start in range(0, width, HD)], axis=0)


def unstack(ref, heads):
    rows, width = ref.shape
    for head in range(width // HD):
        ref[:, head * HD : (head + 1) * HD] = heads[head * rows : (head + 1) * rows]


def probability(queries, keys, segments):
    count = segments.shape[1]
    across = jnp.broadcast_to(segments, (count, count))
    key_at = lax.broadcasted_iota(jnp.int32, (count, count), 0)
    query_at = lax.broadcasted_iota(jnp.int32, (count, count), 1)
    allowed = (across == across.T) & (key_at <= query_at)
    allowed = jnp.concatenate([allowed] * (queries.shape[0] // count), axis=1)
    scores = jnp.where(allowed, contract(keys, queries, 1, 1) * SCALE, -jnp.inf)
    weights = jnp.exp(scores - jnp.max(scores, axis=0, keepdims=True))
    return weights * (1.0 / jnp.sum(weights, axis=0, keepdims=True))


def forward_kernel(q_ref, k_ref, v_ref, segments_ref, held_q_ref, held_k_ref, held_v_ref, out_ref, stash_ref, fresh_ref):
    rows, width = q_ref.shape
    prob = probability(stacked(q_ref, width), k_ref[...], segments_ref[...])
    stash_ref[:, :width] = held_q_ref[...]
    stash_ref[:, width : width + HD] = held_k_ref[...]
    stash_ref[:, width + HD : width + 2 * HD] = held_v_ref[...]
    stash_ref[:, width + 2 * HD :] = k_ref[...]
    fresh_ref[...] = v_ref[...]
    unstack(out_ref, contract(prob.astype(jnp.bfloat16), v_ref[...], 0, 0).astype(jnp.bfloat16))


def backward_kernel(stash_ref, grad_ref, segments_ref, grad_q_ref, grad_k_ref, grad_v_ref, fresh_k_ref):
    width = grad_ref.shape[1]
    fresh_k_ref[...] = stash_ref[:, width + 2 * HD :]
    queries, grads = stacked(stash_ref, width), stacked(grad_ref, width)
    keys, values = stash_ref[:, width : width + HD], stash_ref[:, width + HD : width + 2 * HD]
    prob = probability(queries, keys, segments_ref[...])
    dprob = contract(values, grads, 1, 1)
    delta = jnp.sum(prob * dprob, axis=0, keepdims=True)
    dscore = (prob * (dprob - delta) * SCALE).astype(jnp.bfloat16)
    grad_v_ref[...] = contract(prob.astype(jnp.bfloat16), grads, 1, 0).astype(jnp.bfloat16)
    grad_k_ref[...] = contract(dscore, queries, 1, 0).astype(jnp.bfloat16)
    unstack(grad_q_ref, contract(dscore, keys, 0, 0).astype(jnp.bfloat16))


def like(rows, columns):
    return jax.ShapeDtypeStruct((rows, columns), jnp.bfloat16)


def finish_kernel(pieces_ref, early_ref, late_ref, fresh_ref, passed_ref, q_ref, v_ref):
    parts, _, width = pieces_ref.shape
    late = jnp.where(lax.rem(lax.axis_index("section"), 16) == 0, parts - 2, 0)
    for part in range(parts):
        column = pl.multiple_of(lax.rem(part + late, parts) * width, width)
        passed_ref[:, pl.ds(column, width)] = pieces_ref[part]
    v_ref[...] = fresh_ref[...]
    is_early = lax.axis_index("tp") < 2

    @pl.when(is_early)
    def _():
        q_ref[...] = early_ref[...]

    @pl.when(jnp.logical_not(is_early))
    def _():
        q_ref[...] = late_ref[...]


def finish(pieces, early, late, fresh):
    parts, rows, width = pieces.shape
    tokens = early.shape[0]
    arrays = (pltpu.with_memory_space_constraint(x, pltpu.VMEM) for x in (pieces, early, late, fresh))
    return pl.pallas_call(
        finish_kernel,
        out_shape=(like(rows, parts * width), like(tokens, width), like(tokens, HD)),
        in_specs=[VMEM] * 4,
        out_specs=(VMEM,) * 3,
        cost_estimate=pl.CostEstimate(flops=0, bytes_accessed=8 * parts * rows * width, transcendentals=0),
        name="finish",
    )(*arrays)


def handed_on(value):
    count, parts = lax.axis_size("section"), lax.axis_size("tp")
    pairs = []
    for section in range(count):
        after = (section + 1) % count
        late = {0: 2}.get(after % 16, 0)
        pairs += [(section * parts + t, after * parts + (t + late) % parts) for t in range(parts)]
    return lax.ppermute(value, ("section", "tp"), pairs)


def held_in_vmem(rows, columns):
    return pltpu.VMEM((rows, columns), jnp.bfloat16)


def forward(q, k, v, segments, held_q, held_k, held_v):
    rows, width = q.shape
    whole = width + 2 * HD
    return pl.pallas_call(
        forward_kernel,
        out_shape=(held_in_vmem(rows, width), held_in_vmem(rows, whole + HD), held_in_vmem(rows, HD)),
        in_specs=[VMEM] * 7,
        out_specs=(VMEM,) * 3,
        cost_estimate=pl.CostEstimate(flops=FORWARD_FLOPS * rows * rows * width, bytes_accessed=20 * rows * width, transcendentals=rows * width),
        name="forward",
    )(q, k, v, segments, held_q, held_k, held_v)


def backward(stash, grad, segments):
    rows, width = grad.shape
    return pl.pallas_call(
        backward_kernel,
        out_shape=(like(rows, width),) + (like(rows, HD),) * 3,
        in_specs=[VMEM] * 3,
        out_specs=(VMEM,) * 4,
        cost_estimate=pl.CostEstimate(flops=BACKWARD_FLOPS * rows * rows * width, bytes_accessed=8 * rows * width, transcendentals=rows * width),
        name="backward",
    )(pltpu.with_memory_space_constraint(stash, pltpu.VMEM), pltpu.with_memory_space_constraint(grad, pltpu.VMEM), segments)


def shifted(value, steps):
    count = lax.axis_size("section")
    return lax.ppermute(value, "section", [(i, (i + steps) % count) for i in range(count)])


def mirrored(value, lines=None):
    count, parts = lax.axis_size("section"), lax.axis_size("tp")
    if lines is None:
        return lax.ppermute(value, "section", [(i, count - 1 - i) for i in range(count)])
    pairs = [(i * parts + t, (count - 1 - i) * parts + t) for i in range(count) for t in range(parts) if t // 2 in lines]
    return lax.ppermute(value, ("section", "tp"), pairs)


def shards(fwd_q, fwd_k, fwd_v, fwd_segments, held_q, held_k, held_v, back_segments, up_grad):
    arriving = shifted(up_grad[0], -1)
    out, stash, fresh = forward(fwd_q[0], fwd_k[0], fwd_v[0], fwd_segments, held_q[0], held_k[0], held_v[0])
    parts = lax.axis_size("tp")
    out = handed_on(out).reshape(parts, out.shape[0] // parts, out.shape[1])
    stash = mirrored(stash)
    lines = range(lax.axis_size("tp") // 2)
    early_q = mirrored(fwd_q[0], lines[:1])
    pieces = lax.all_to_all(out, "tp", split_axis=0, concat_axis=0)
    late_q = mirrored(fwd_q[0], lines[1:])
    stash, early_q = lax.optimization_barrier((stash, early_q))
    grad_q, grad_k, grad_v, evicted_k = backward(stash, arriving, back_segments)
    late_q, fresh, grad_k = lax.optimization_barrier((late_q, mirrored(fresh), grad_k))
    passed, evicted_q, evicted_v = finish(pieces, early_q, late_q, fresh)
    return tuple(x[None] for x in (passed, evicted_q, evicted_k, evicted_v, grad_q, grad_k, grad_v))


def solution(mesh):
    heads, tokens = P("section", None, "tp"), P("section", "tp", None)
    segments = P("section", None)
    in_specs = (heads, heads, heads, segments, heads, heads, heads, segments, heads)
    out_specs = (tokens, heads, heads, heads, heads, heads, heads)
    return jax.shard_map(shards, mesh=mesh, in_specs=in_specs, out_specs=out_specs, check_vma=False)
```
